256 devices in a mesh: dom: 16 (over x, y_lo, core), grp: 16 (over z, y_hi).
Axes of the slice: x: 4, y: 4 (y_hi: 2, y_lo: 2; y = y_hi * 2 + y_lo), z: 8, core: 2. Of those that a mesh axis runs over, the one named last changes fastest.
Arguments:
- interface_panel: bfloat16 [4096, 512], P('dom'), may hold values from -6 to 6
- interface_block: bfloat16 [4096, 256], P('dom'), may hold values from -0.375 to 0.375
- coupling: bfloat16 [16, 16384, 4096], P('dom', 'grp'), may hold values from -0.09375 to 0.09375
- coupling_pattern: int32 [16, 32, 16], P('dom', 'grp'), may hold values from 0 to 1, as said below
- tile_ranks: int32 [16, 32], P('dom', 'grp'), may hold values from 16 to 64
- basis_left: bfloat16 [16, 64, 16384], P('dom', None, 'grp'), may hold values from -0.75 to 0.75
- basis_right: bfloat16 [16, 64, 16384], P('dom', None, 'grp'), may hold values from -0.046875 to 0.046875
- interior_scale: float32 [16, 16384], P('dom', 'grp'), may hold values from 0.5 to 2
Outputs:
- schur_image: float32 [4096, 512], P('dom')
The draws below stay inside these ranges and needn't reach their ends.
Inputs may be any that keep to these rules, and one draw needn't show every extreme that they name: `coupling_pattern`: each subdomain couples every tile to its own interface block; subdomains differ in how many blocks their tiles couple to.
All inputs are finite; a program needn't handle non-finite values.
Results may differ from the reference program's by a relative error of at most 0.00047.
Values may be sent and summed in bfloat16 or wider, within the bound.
No kernel may reach another device: no remote copies, remote signals or barrier semaphores. Data moves between devices by JAX's collectives and lax.ppermute only.
A program may use at most 64 MiB of HBM per device.

```python
import jax
import jax.numpy as jnp
from jax import lax

G = 4096
TILE = 512
RANK = 64
R = 512
TILES = 32
NI = 16384
GB = 256
N_DOM = 16


def draw_coupling_pattern(key, part):
    key = jax.random.fold_in(key, 11)
    first_key, second_key = jax.random.split(key)
    density = jax.random.randint(first_key, (N_DOM, 1, 1), 2, N_DOM + 1)
    scores = jax.random.randint(second_key, (N_DOM, TILES, N_DOM), 0, N_DOM)
    pattern = (scores < density).astype(jnp.int32)
    domain_index = jnp.arange(N_DOM, dtype=jnp.int32)
    own_block = (domain_index[:, None, None] == domain_index[None, None, :]).astype(jnp.int32)
    pattern = jnp.maximum(pattern, own_block)
    next_block = (domain_index[None, :] == (domain_index[:, None] + 1) % N_DOM).astype(jnp.int32)
    pattern = pattern.at[:, 0, :].set(pattern[:, 0, :] * (1 - next_block))
    return pattern


def draw_tile_ranks(key, part):
    key = jax.random.fold_in(key, 23)
    ranks = jax.random.randint(key, (N_DOM, TILES), RANK // 4, RANK + 1)
    ranks = ranks.at[0, 0].set(RANK)
    ranks = ranks.at[0, 1].set(RANK // 4)
    return ranks.astype(jnp.int32)


def block_levels(own_key, extent, cuts, least, largest):
    gain = 1.0
    for position, blocks in cuts:
        heights = jax.random.uniform(jax.random.fold_in(jax.random.fold_in(own_key, 6), position), (blocks,), jnp.float32, least / len(cuts), largest / len(cuts))
        gain = gain * jnp.repeat(jnp.exp(heights), extent[position] // blocks).reshape((-1,) + (1,) * (len(extent) - 1 - position))
    return gain


def scatter_about(key, dims, scale, bound, shards=(), held_as=jnp.bfloat16):
    factor_of = block_levels(key, dims, shards, -0.22, 0.18) if shards else 1.0
    result = jax.random.normal(key, dims, jnp.float32) * scale * factor_of
    return jnp.minimum(jnp.maximum(result, -bound), bound).astype(held_as)


def setup_inputs(seed: int = 0) -> dict:
    key_of = jax.random.split(jax.random.key(seed), 9)
    interface_panel = scatter_about(key_of[0], (G, R), 1.0, 6.0, ((0, 16),))
    interface_block = scatter_about(key_of[1], (G, GB), GB ** -0.5, 0.375, ((0, 16),))
    coupling = scatter_about(key_of[2], (N_DOM, NI, G), G ** -0.5, 0.09375, ((0, 16), (1, 16)))
    coupling_pattern = draw_coupling_pattern(jax.random.fold_in(key_of[8], 71), 0)
    tile_ranks = draw_tile_ranks(jax.random.fold_in(key_of[8], 71), 0)
    basis_left = scatter_about(key_of[5], (N_DOM, RANK, NI), RANK ** -0.5, 0.75, ((0, 16), (2, 16)))
    basis_right = scatter_about(key_of[6], (N_DOM, RANK, NI), NI ** -0.5, 0.046875, ((0, 16), (2, 16)))
    interior_scale = jnp.clip(0.5 + 1.5 * jax.random.uniform(key_of[7], (N_DOM, NI), jnp.float32) ** block_levels(key_of[7], (N_DOM, NI), ((0, 16), (1, 16)), -0.2, 0.2), 0.5, 2.0)
    return {"interface_panel": interface_panel, "interface_block": interface_block, "coupling": coupling, "coupling_pattern": coupling_pattern, "tile_ranks": tile_ranks, "basis_left": basis_left, "basis_right": basis_right, "interior_scale": interior_scale}


def reference(interface_panel, interface_block, coupling, coupling_pattern, tile_ranks, basis_left, basis_right, interior_scale):
    block_rows = G // N_DOM

    def one_domain(running, index):
        pattern_now = coupling_pattern[index]
        column_mask = jnp.repeat(pattern_now, block_rows, axis=1).astype(jnp.bfloat16)
        masked = (coupling[index].reshape(TILES, TILE, G) * column_mask[:, None, :]).reshape(TILES * TILE, G)
        load = jnp.dot(masked, interface_panel, preferred_element_type=jnp.float32)
        rank_mask = (jnp.arange(RANK, dtype=jnp.int32)[:, None] < tile_ranks[index][None, :]).astype(jnp.float32)
        right_part = basis_right[index].astype(jnp.float32).reshape(RANK, TILES, TILE) * rank_mask[:, :, None]
        left_part = basis_left[index].astype(jnp.float32).reshape(RANK, TILES, TILE) * rank_mask[:, :, None]
        load_tiles = load.reshape(TILES, TILE, R)
        projection = jnp.einsum("kti,tir->kr", right_part, load_tiles, precision=lax.Precision.HIGHEST)
        solved = interior_scale[index].reshape(TILES, TILE)[:, :, None] * load_tiles
        solved = solved + jnp.einsum("kti,kr->tir", left_part, projection, precision=lax.Precision.HIGHEST)
        solved = solved.reshape(TILES * TILE, R).astype(jnp.bfloat16)
        back_term = lax.dot_general(masked, solved, (((0,), (0,)), ((), ())), preferred_element_type=jnp.float32)
        return running + back_term, None

    coupled, unused = lax.scan(one_domain, jnp.zeros((G, R), jnp.float32), jnp.arange(N_DOM, dtype=jnp.int32))
    diag_blocks = interface_block.reshape(N_DOM, block_rows, block_rows).astype(jnp.float32)
    panel_blocks = interface_panel.reshape(N_DOM, block_rows, R).astype(jnp.float32)
    local_image = jnp.einsum("dij,djr->dir", diag_blocks, panel_blocks, precision=lax.Precision.HIGHEST).reshape(G, R)
    return local_image - coupled
```

```python
import functools

import jax
import jax.numpy as jnp
from jax import lax
from jax.experimental import pallas as pl
from jax.experimental.pallas import tpu as pltpu
from jax.sharding import PartitionSpec as P

TILE = 512
RANK = 64
BLOCK = 256
SLAB = 256
BF16 = jnp.bfloat16
F32 = jnp.float32
VMEM_BYTES = 48 * 1024 * 1024


def split3(value):
    high = value.astype(BF16)
    rest = value - high.astype(F32)
    middle = rest.astype(BF16)
    low = (rest - middle.astype(F32)).astype(BF16)
    return high, middle, low


def masked_columns(coupling_ref, pattern_ref, tile, parity, blocks):
    pieces = []
    for k in range(blocks):
        block = 2 * k + parity
        columns = coupling_ref[:, pl.ds(pl.multiple_of(block * BLOCK, BLOCK), BLOCK)]
        keep = pattern_ref[tile, block].astype(F32)
        pieces.append(columns * jnp.broadcast_to(keep, columns.shape).astype(BF16))
    return jnp.concatenate(pieces, axis=1)


def load_first_kernel(core_ref, pattern_ref, coupling_ref, panel_ref, load_ref, *, blocks):
    tile = pl.program_id(0) // (TILE // SLAB)
    lhs = masked_columns(coupling_ref, pattern_ref, tile, core_ref[0], blocks)
    load_ref[...] = jnp.dot(lhs, panel_ref[...], preferred_element_type=F32)


def load_second_kernel(
    core_ref, pattern_ref, ranks_ref, coupling_ref, panel_ref, first_ref, right_ref,
    load_ref, projection_ref, *, blocks,
):
    step = pl.program_id(0)
    tile = step // (TILE // SLAB)
    lhs = masked_columns(coupling_ref, pattern_ref, tile, 1 - core_ref[0], blocks)
    load = first_ref[...] + jnp.dot(lhs, panel_ref[...], preferred_element_type=F32)
    load_ref[...] = load
    row = lax.broadcasted_iota(jnp.int32, right_ref.shape, 0)
    right = jnp.where(row < ranks_ref[tile], right_ref[...], jnp.zeros_like(right_ref))
    part = 0.0
    for piece in split3(load):
        part = part + jnp.dot(right, piece, preferred_element_type=F32)

    @pl.when(step == 0)
    def _():
        projection_ref[...] = part

    @pl.when(step > 0)
    def _():
        projection_ref[...] += part


def solve_kernel(ranks_ref, load_ref, left_ref, scale_ref, projection_ref, solved_ref):
    tile = pl.program_id(0) // (TILE // SLAB)
    row = lax.broadcasted_iota(jnp.int32, left_ref.shape, 0)
    left = jnp.where(row < ranks_ref[tile], left_ref[...], jnp.zeros_like(left_ref))
    lefts = jnp.concatenate([left] * 3, axis=0)
    pieces = jnp.concatenate(split3(projection_ref[...]), axis=0)
    low_rank = lax.dot_general(
        pieces, lefts, (((0,), (0,)), ((), ())), preferred_element_type=F32
    )
    solved_ref[...] = (scale_ref[...] * load_ref[...].T + low_rank).astype(BF16)


def back_kernel(core_ref, pattern_ref, solved_ref, *refs, other, blocks, add):
    coupling_refs = refs[:blocks]
    out_ref = refs[-1]
    core = core_ref[0]
    parity = 1 - core if other else core
    tiles = pattern_ref.shape[0]
    base = refs[-2] if add else None
    offset = pl.program_id(0)
    for k in range(blocks):
        block = 2 * (offset * blocks + k) + parity
        block = block + core_ref[1]
        pieces = []
        for tile in range(tiles):
            keep = pattern_ref[tile, block].astype(F32)
            rows = coupling_refs[k][tile * TILE : (tile + 1) * TILE, :]
            pieces.append(rows * jnp.broadcast_to(keep, rows.shape).astype(BF16))
        rhs = jnp.concatenate(pieces, axis=0)
        value = jnp.dot(solved_ref[...], rhs, preferred_element_type=F32)
        if add:
            value = value + base[k].astype(F32)
        out_ref[k] = value.astype(BF16)


def params():
    return pltpu.CompilerParams(vmem_limit_bytes=VMEM_BYTES)


def load_first(core, pattern, coupling, panel):
    rows, width = coupling.shape
    depth, vectors = panel.shape
    blocks = depth // BLOCK
    return pl.pallas_call(
        functools.partial(load_first_kernel, blocks=blocks),
        out_shape=jax.ShapeDtypeStruct((rows, vectors), F32),
        grid_spec=pltpu.PrefetchScalarGridSpec(
            num_scalar_prefetch=2,
            grid=(rows // SLAB,),
            in_specs=[
                pl.BlockSpec((SLAB, width), lambda i, *_: (i, 0)),
                pl.BlockSpec((depth, vectors), lambda i, *_: (0, 0)),
            ],
            out_specs=pl.BlockSpec((SLAB, vectors), lambda i, *_: (i, 0)),
        ),
        cost_estimate=pl.CostEstimate(
            flops=2 * rows * depth * vectors, bytes_accessed=12 << 20, transcendentals=0
        ),
        compiler_params=params(),
        name="load_first",
    )(core, pattern, coupling, panel)


def load_second(core, pattern, ranks, coupling, panel, first, right):
    rows, width = coupling.shape
    depth, vectors = panel.shape
    blocks = depth // BLOCK
    return pl.pallas_call(
        functools.partial(load_second_kernel, blocks=blocks),
        out_shape=(
            jax.ShapeDtypeStruct((rows, vectors), F32),
            jax.ShapeDtypeStruct((RANK, vectors), F32),
        ),
        grid_spec=pltpu.PrefetchScalarGridSpec(
            num_scalar_prefetch=3,
            grid=(rows // SLAB,),
            in_specs=[
                pl.BlockSpec((SLAB, width), lambda i, *_: (i, 0)),
                pl.BlockSpec((depth, vectors), lambda i, *_: (0, 0)),
                pl.BlockSpec((SLAB, vectors), lambda i, *_: (i, 0)),
                pl.BlockSpec((RANK, SLAB), lambda i, *_: (0, i)),
            ],
            out_specs=(
                pl.BlockSpec((SLAB, vectors), lambda i, *_: (i, 0)),
                pl.BlockSpec((RANK, vectors), lambda i, *_: (0, 0)),
            ),
        ),
        cost_estimate=pl.CostEstimate(
            flops=2 * rows * depth * vectors, bytes_accessed=16 << 20, transcendentals=0
        ),
        compiler_params=params(),
        name="load_second",
    )(core, pattern, ranks, coupling, panel, first, right)


def solve(ranks, load, left, scale, projection):
    rows, vectors = load.shape
    return pl.pallas_call(
        solve_kernel,
        out_shape=jax.ShapeDtypeStruct((vectors, rows), BF16),
        grid_spec=pltpu.PrefetchScalarGridSpec(
            num_scalar_prefetch=1,
            grid=(rows // SLAB,),
            in_specs=[
                pl.BlockSpec((SLAB, vectors), lambda i, *_: (i, 0)),
                pl.BlockSpec((RANK, SLAB), lambda i, *_: (0, i)),
                pl.BlockSpec((1, SLAB), lambda i, *_: (0, i)),
                pl.BlockSpec((RANK, vectors), lambda i, *_: (0, 0)),
            ],
            out_specs=pl.BlockSpec((vectors, SLAB), lambda i, *_: (0, i)),
        ),
        compiler_params=params(),
        name="solve",
    )(ranks, load, left, scale, projection)


def back(core, pattern, solved, coupling, other, start, count, received=None):
    vectors, rows = solved.shape
    per_step = 2
    scalars = jnp.stack([core, jnp.int32(2 * start)])

    def column_block(k):
        def index(i, core_ref, pattern_ref):
            parity = 1 - core_ref[0] if other else core_ref[0]
            return 0, 2 * (i * per_step + k) + parity + core_ref[1]

        return index

    add = received is not None
    in_specs = [pl.BlockSpec((vectors, rows), lambda i, *_: (0, 0))]
    in_specs += [pl.BlockSpec((rows, BLOCK), column_block(k)) for k in range(per_step)]
    operands = [solved] + [coupling] * per_step
    step_spec = pl.BlockSpec((per_step, vectors, BLOCK), lambda i, *_: (i, 0, 0))
    if add:
        in_specs.append(step_spec)
        operands.append(received)
    return pl.pallas_call(
        functools.partial(back_kernel, other=other, blocks=per_step, add=add),
        out_shape=jax.ShapeDtypeStruct((count, vectors, BLOCK), BF16),
        grid_spec=pltpu.PrefetchScalarGridSpec(
            num_scalar_prefetch=2,
            grid=(count // per_step,),
            in_specs=in_specs,
            out_specs=step_spec,
        ),
        cost_estimate=pl.CostEstimate(
            flops=2 * rows * count * BLOCK * vectors, bytes_accessed=6 << 20, transcendentals=0
        ),
        compiler_params=params(),
        name="back",
    )(scalars, pattern, *operands)


def exchange(value, axes):
    return lax.all_to_all(value, axes, 0, 0, tiled=True)


def swap(value):
    return lax.ppermute(value, "c", [(0, 1), (1, 0)])


def local(
    interface_panel,
    interface_block,
    coupling,
    coupling_pattern,
    tile_ranks,
    basis_left,
    basis_right,
    interior_scale,
):
    near = lax.axis_size("x") * lax.axis_size("yl")
    halves = lax.axis_size("yh")
    layers = lax.axis_size("z")
    block_rows, vectors = interface_panel.shape
    core_index = lax.axis_index("c").astype(jnp.int32)
    core = core_index[None]
    pattern, ranks = coupling_pattern[0], tile_ranks[0]
    masked_source = coupling[0]

    mine = jnp.broadcast_to(interface_panel[None], (near, block_rows, vectors))
    mine = exchange(mine, ("x", "yl")).reshape(near * block_rows, vectors)
    theirs = swap(mine)
    first = load_first(core, pattern, masked_source, mine)
    load, partial = load_second(
        core, pattern, ranks, masked_source, theirs, first, basis_right[0]
    )

    members = layers * halves
    partial = exchange(partial.reshape(members, RANK // members, vectors), ("yh", "z"))
    summed = jnp.sum(partial, axis=0)
    projection = exchange(
        jnp.broadcast_to(summed[None], (members,) + summed.shape), ("yh", "z")
    ).reshape(RANK, vectors)

    solved = solve(ranks, load, basis_left[0], interior_scale, projection)

    half = near // 2
    give_a = swap(back(core_index, pattern, solved, masked_source, True, 0, half))
    give_b = swap(back(core_index, pattern, solved, masked_source, True, half, half))
    keep_a = back(core_index, pattern, solved, masked_source, False, 0, half, give_a)
    keep_b = back(core_index, pattern, solved, masked_source, False, half, half, give_b)
    terms = jnp.concatenate([keep_a, keep_b], axis=0)

    part = vectors // halves
    terms = exchange(terms.reshape(near * halves, part, block_rows), ("x", "yl", "yh"))
    terms = jnp.sum(terms.astype(F32), axis=0)
    piece = part // layers
    terms = exchange(terms.reshape(layers, piece, block_rows), "z")
    terms = jnp.sum(terms, axis=0)
    terms = exchange(jnp.broadcast_to(terms[None], (members, piece, block_rows)), ("yh", "z"))
    coupled = terms.reshape(vectors, block_rows).T

    local_image = jnp.dot(interface_block, interface_panel, preferred_element_type=F32)
    return local_image - coupled


def solution(mesh):
    shape = (4, 2, 2, 8, 2)
    fine = jax.sharding.Mesh(mesh.devices.reshape(shape), ("x", "yl", "c", "z", "yh"))
    dom, grp = ("x", "yl", "c"), ("z", "yh")
    return jax.shard_map(
        local,
        mesh=fine,
        in_specs=(
            P(dom, None),
            P(dom, None),
            P(dom, grp, None),
            P(dom, grp, None),
            P(dom, grp),
            P(dom, None, grp),
            P(dom, None, grp),
            P(dom, grp),
        ),
        out_specs=P(dom, None),
        check_vma=False,
    )
```

```python
import functools

import jax
import jax.numpy as jnp
from jax import lax
from jax.experimental import pallas as pl
from jax.experimental.pallas import tpu as pltpu
from jax.sharding import PartitionSpec as P

TILE = 512
RANK = 64
BLOCK = 256
SLAB = 256
BF16 = jnp.bfloat16
F32 = jnp.float32
VMEM_BYTES = 20 * 1024 * 1024


def split3(value):
    high = value.astype(BF16)
    rest = value - high.astype(F32)
    middle = rest.astype(BF16)
    low = (rest - middle.astype(F32)).astype(BF16)
    return high, middle, low


def rank_masked(basis, rank):
    row = lax.broadcasted_iota(jnp.int32, basis.shape, 0)
    return jnp.where(row < rank, basis, jnp.zeros_like(basis))


STEPS = ((0, 0), (0, 1), (-1, 0), (1, 0), (2, 0), (-1, 1), (1, 1), (2, 1))


def owned_block(step, same_core):
    wide, high = lax.axis_size("x"), lax.axis_size("yl")
    x = lax.rem(lax.axis_index("x") + (step[0] + wide), wide)
    y = lax.rem(lax.axis_index("yl") + (step[1] + high), high)
    core = lax.axis_index("c")
    return (x * high + y) * 2 + (core if same_core else 1 - core)


def mask_kernel(
    pattern_ref, ranks_ref, coupling_ref, right_ref, left_ref,
    own_ref, other_ref, own_fold_ref, other_fold_ref, left_out_ref, fold_ref,
):
    step = pl.program_id(0)
    tile = step // (TILE // SLAB)
    rank = ranks_ref[tile]
    left = rank_masked(left_ref[...], rank)
    left_out_ref[...] = jnp.concatenate([left] * 3, axis=0)
    right = rank_masked(right_ref[...], rank)

    @pl.when(step == 0)
    def _():
        fold_ref[...] = jnp.zeros_like(fold_ref)

    for index, out_ref in enumerate((own_ref, other_ref)):
        blocks = out_ref.shape[1] // BLOCK
        for k in range(blocks):
            block = owned_block(STEPS[k], index == 0)
            columns = coupling_ref[:, pl.ds(pl.multiple_of(block * BLOCK, BLOCK), BLOCK)]
            keep = pattern_ref[tile, block].astype(F32)
            keep = jnp.broadcast_to(keep, columns.shape).astype(BF16)
            out_ref[:, k * BLOCK : (k + 1) * BLOCK] = columns * keep
        fold_ref[index] += jnp.dot(right, out_ref[...], preferred_element_type=F32)

    @pl.when(step == pl.num_programs(0) - 1)
    def _():
        own_fold_ref[...] = jnp.concatenate(split3(fold_ref[0]), axis=0)
        other_fold_ref[...] = jnp.concatenate(split3(fold_ref[1]), axis=0)


def stacked(refs):
    return jnp.concatenate([ref[...] for ref in refs], axis=0)


def project_kernel(own_fold_ref, other_fold_ref, *refs):
    out_ref, panel_refs = refs[-1], refs[:-1]
    half = len(panel_refs) // 2
    value = jnp.dot(own_fold_ref[...], stacked(panel_refs[:half]), preferred_element_type=F32)
    value += jnp.dot(
        other_fold_ref[...], stacked(panel_refs[half:]), preferred_element_type=F32
    )
    out_ref[...] = value[:RANK] + (value[RANK : 2 * RANK] + value[2 * RANK :])


def load_first_kernel(masked_ref, *refs):
    out_ref, token_ref = refs[-2:]
    token_ref[...] = jnp.zeros_like(token_ref)
    panel = stacked(refs[:-2])
    for tile in range(out_ref.shape[0] // TILE):
        rows = slice(tile * TILE, (tile + 1) * TILE)
        out_ref[rows, :] = jnp.dot(masked_ref[rows, :], panel, preferred_element_type=F32)


def load_second_kernel(masked_ref, first_ref, scale_ref, *refs):
    out_ref, token_ref = refs[-2:]
    token_ref[...] = jnp.zeros_like(token_ref)
    panel = stacked(refs[:-2])
    for tile in range(first_ref.shape[0] // TILE):
        rows = slice(tile * TILE, (tile + 1) * TILE)
        load = jnp.dot(masked_ref[rows, :], panel, preferred_element_type=F32)
        out_ref[:, rows] = scale_ref[:, rows] * (first_ref[rows, :] + load).T


def back_block(solved_ref, masked_ref, block):
    masked = masked_ref[:, block * BLOCK : (block + 1) * BLOCK]
    return jnp.dot(solved_ref[...], masked, preferred_element_type=F32)


def solve_back_kernel(
    scaled_ref, projection_ref, left_ref, masked_ref, solved_ref, out_ref
):
    pieces = jnp.concatenate(split3(projection_ref[...]), axis=0)
    low_rank = lax.dot_general(
        pieces, left_ref[...], (((0,), (0,)), ((), ())), preferred_element_type=F32
    )
    solved_ref[...] = (scaled_ref[...] + low_rank).astype(BF16)
    for k in range(out_ref.shape[0]):
        out_ref[k] = back_block(solved_ref, masked_ref, k).astype(BF16)


def back_kernel(solved_ref, masked_ref, out_ref, *, start):
    for k in range(out_ref.shape[0]):
        out_ref[k] = back_block(solved_ref, masked_ref, start + k).astype(BF16)


def back_add_kernel(solved_ref, masked_ref, given_ref, *refs, start):
    out_ref = refs[-1]
    for k in range(given_ref.shape[0]):
        value = back_block(solved_ref, masked_ref, start + k) + given_ref[k].astype(F32)
        owner = lax.div(owned_block(STEPS[start + k], True), 2)
        out_ref[owner] = value.astype(BF16)


def params():
    return pltpu.CompilerParams(vmem_limit_bytes=VMEM_BYTES)


def cost(flops, size):
    return pl.CostEstimate(flops=flops, bytes_accessed=size, transcendentals=0)


def whole(shape):
    return pl.BlockSpec(shape, lambda *_: (0,) * len(shape), pipeline_mode=pl.Buffered(1))


ANYWHERE = pl.BlockSpec(memory_space=pl.ANY)
INSIDE = pl.BlockSpec(memory_space=pltpu.VMEM)


def far(value):
    return pltpu.with_memory_space_constraint(value, pltpu.HBM)


def near_by(value):
    return pltpu.with_memory_space_constraint(value, pltpu.VMEM)


def mask(pattern, ranks, coupling, right, left):
    rows, width = coupling.shape
    half = width // 2
    masked = jax.ShapeDtypeStruct((rows, half), BF16)
    fold = jax.ShapeDtypeStruct((3 * RANK, half), BF16)
    masked_spec = pl.BlockSpec((SLAB, half), lambda i, *_: (i, 0))
    basis_spec = pl.BlockSpec((RANK, SLAB), lambda i, *_: (0, i))
    return pl.pallas_call(
        mask_kernel,
        out_shape=(
            masked, masked, fold, fold, jax.ShapeDtypeStruct((3 * RANK, rows), BF16)
        ),
        grid_spec=pltpu.PrefetchScalarGridSpec(
            num_scalar_prefetch=2,
            grid=(rows // SLAB,),
            in_specs=[
                pl.BlockSpec((SLAB, width), lambda i, *_: (i, 0)), basis_spec, basis_spec
            ],
            out_specs=(
                masked_spec,
                masked_spec,
                whole(fold.shape),
                whole(fold.shape),
                pl.BlockSpec((3 * RANK, SLAB), lambda i, *_: (0, i)),
            ),
            scratch_shapes=[pltpu.VMEM((2, RANK, half), F32)],
        ),
        cost_estimate=cost(2 * rows * width * RANK, 4 * rows * width),
        compiler_params=params(),
        name="mask",
    )(far(pattern), far(ranks), far(coupling), far(right), far(left))


def inside(kernel, name, out_shape, operands, flops, aliases=None):
    return pl.pallas_call(
        kernel,
        out_shape=out_shape,
        in_specs=[INSIDE] * len(operands),
        out_specs=jax.tree.map(lambda _: INSIDE, out_shape),
        input_output_aliases=aliases or {},
        cost_estimate=cost(flops, 1 << 20),
        compiler_params=params(),
        name=name,
    )(*[near_by(operand) for operand in operands])


def project(own_fold, other_fold, mine, theirs):
    vectors = mine[0].shape[1]
    return inside(
        project_kernel, "project", jax.ShapeDtypeStruct((RANK, vectors), F32),
        (own_fold, other_fold, *mine, *theirs), 12 * own_fold.size * vectors,
    )


def load_first(masked, panels):
    rows, depth = masked.shape
    vectors = panels[0].shape[1]
    out = jax.ShapeDtypeStruct((rows, vectors), F32)
    token = jax.ShapeDtypeStruct((RANK, vectors), F32)
    return inside(
        load_first_kernel, "load_first", (out, token), (masked, *panels),
        2 * rows * depth * vectors,
    )


def load_second(masked, panels, first, scale):
    rows, depth = masked.shape
    vectors = panels[0].shape[1]
    out = jax.ShapeDtypeStruct((vectors, rows), F32)
    token = jax.ShapeDtypeStruct((RANK, vectors), F32)
    return inside(
        load_second_kernel, "load_second", (out, token), (masked, first, scale, *panels),
        2 * rows * depth * vectors,
    )


def solve_back(scaled, projection, left, masked, count):
    vectors, rows = scaled.shape
    out = (
        jax.ShapeDtypeStruct((vectors, rows), BF16),
        jax.ShapeDtypeStruct((count, vectors, BLOCK), BF16),
    )
    return inside(
        solve_back_kernel, "solve_back", out, (scaled, projection, left, masked),
        2 * rows * count * BLOCK * vectors,
    )


def back(solved, masked, start, count):
    vectors, rows = solved.shape
    return inside(
        functools.partial(back_kernel, start=start), "back",
        jax.ShapeDtypeStruct((count, vectors, BLOCK), BF16), (solved, masked),
        2 * rows * count * BLOCK * vectors,
    )


def back_add(solved, masked, start, given, into):
    vectors, rows = solved.shape
    return inside(
        functools.partial(back_add_kernel, start=start), "back_add",
        jax.ShapeDtypeStruct((len(STEPS), vectors, BLOCK), BF16),
        (solved, masked, given, *into), 2 * rows * given.shape[0] * BLOCK * vectors,
        {3: 0} if into else None,
    )


def exchange(value, axes):
    return lax.all_to_all(value, axes, 0, 0, tiled=True)


def swap(value):
    return lax.ppermute(value, "c", [(0, 1), (1, 0)])


def pin_kernel(*refs):
    pass


def pin(values, after):
    shapes = [jax.ShapeDtypeStruct(value.shape, value.dtype) for value in values]
    return pl.pallas_call(
        pin_kernel,
        out_shape=shapes,
        in_specs=[ANYWHERE] * (len(values) + 1),
        out_specs=[ANYWHERE] * len(values),
        input_output_aliases={k: k for k in range(len(values))},
        compiler_params=params(),
        name="pin",
    )(*values, after)


def shift(value, dx, dy, dh=0):
    wide, high, halves = [lax.axis_size(name) for name in ("x", "yl", "yh")]
    pairs = [
        (
            (x * high + y) * halves + h,
            ((x + dx) % wide * high + (y + dy) % high) * halves + (h + dh) % halves,
        )
        for x in range(wide)
        for y in range(high)
        for h in range(halves)
    ]
    return lax.ppermute(value, ("x", "yl", "yh"), pairs)


def sum_round(value, partners, token):
    layers, halves = lax.axis_size("z"), lax.axis_size("yh")
    terms = []
    for dz, dh in partners:
        pairs = [
            (z * halves + h, (z ^ dz) * halves + (h ^ dh))
            for z in range(layers)
            for h in range(halves)
        ]
        terms.append(lax.ppermute(value, ("z", "yh"), pairs))
    return (value + terms[0]) + (terms[1] + terms[2]) + token


def local(
    interface_panel,
    interface_block,
    coupling,
    coupling_pattern,
    tile_ranks,
    basis_left,
    basis_right,
    interior_scale,
):
    members = lax.axis_size("z") * lax.axis_size("yh")
    block_rows, vectors = interface_panel.shape
    here = interface_panel
    behind, ahead, beside = shift(here, 1, 0), shift(here, -1, 0), shift(here, 0, 1)
    across = shift(here, 2, 0)
    own, other, own_fold, other_fold, left = mask(
        coupling_pattern[0], tile_ranks[0], coupling[0], basis_right[0], basis_left[0]
    )
    behind, ahead, beside = pin([behind, ahead, beside], left)
    corners = [shift(behind, 0, 1), shift(ahead, 0, 1, 1), shift(beside, 2, 0)]
    (across,) = pin([across], left)
    mine = [here, beside, behind, ahead, across, *corners]
    theirs = [swap(block) for block in mine]

    projection = project(own_fold, other_fold, mine, theirs)
    first, token_1 = load_first(own, mine)
    scaled, token_2 = load_second(other, theirs, first, interior_scale)
    projection = sum_round(projection, ((1, 0), (0, 1), (1, 1)), token_1)
    projection = sum_round(projection, ((2, 0), (4, 0), (6, 0)), token_2)

    half = len(STEPS) // 2
    solved, give = solve_back(scaled, projection, left, other, half)
    give_1 = swap(give)
    give_2 = swap(back(solved, other, half, half))
    term = back_add(solved, own, 0, give_1, ())
    term = back_add(solved, own, half, give_2, (term,))

    halves, layers = lax.axis_size("yh"), lax.axis_size("z")
    part, piece = vectors // halves, vectors // members
    term = term.reshape(len(STEPS) * halves, part, block_rows)
    term = jnp.sum(exchange(term, ("x", "yl", "yh")).astype(F32), axis=0)
    term = jnp.sum(exchange(term.reshape(layers, piece, block_rows), "z"), axis=0)
    term = exchange(jnp.broadcast_to(term[None], (members, piece, block_rows)), ("yh", "z"))
    coupled = term.reshape(vectors, block_rows).T
    local_image = jnp.dot(interface_block, interface_panel, preferred_element_type=F32)
    return local_image - coupled


def solution(mesh):
    shape = (4, 2, 2, 8, 2)
    fine = jax.sharding.Mesh(mesh.devices.reshape(shape), ("x", "yl", "c", "z", "yh"))
    dom, grp = ("x", "yl", "c"), ("z", "yh")
    return jax.shard_map(
        local,
        mesh=fine,
        in_specs=(
            P(dom, None),
            P(dom, None),
            P(dom, grp, None),
            P(dom, grp, None),
            P(dom, grp),
            P(dom, None, grp),
            P(dom, None, grp),
            P(dom, grp),
        ),
        out_specs=P(dom, None),
        check_vma=False,
    )
```

```python
import functools

import jax
import jax.numpy as jnp
from jax import lax
from jax.experimental import pallas as pl
from jax.experimental.pallas import tpu as pltpu
from jax.sharding import PartitionSpec as P

TILE = 512
RANK = 64
BLOCK = 256
TILES = 2
SLAB = 256
BF16 = jnp.bfloat16
F32 = jnp.float32
VMEM_BYTES = 20 * 1024 * 1024


def split3(value):
    high = value.astype(BF16)
    rest = value - high.astype(F32)
    middle = rest.astype(BF16)
    low = (rest - middle.astype(F32)).astype(BF16)
    return high, middle, low


def rank_masked(basis, rank):
    row = lax.broadcasted_iota(jnp.int32, basis.shape, 0)
    return jnp.where(row < rank, basis, jnp.zeros_like(basis))


STEPS = ((0, 0), (0, 1), (-1, 0), (1, 0), (2, 0), (-1, 1), (1, 1), (2, 1))


def owned_block(step, same_core):
    wide, high = lax.axis_size("x"), lax.axis_size("yl")
    x = lax.rem(lax.axis_index("x") + (step[0] + wide), wide)
    y = lax.rem(lax.axis_index("yl") + (step[1] + high), high)
    core = lax.axis_index("c")
    return (x * high + y) * 2 + (core if same_core else 1 - core)


def mask_kernel(pattern_ref, ranks_ref, coupling_ref, right_ref, left_ref, *refs, tile, last):
    own_ref, other_ref, left_out_ref, *fold_out_refs, fold_ref = refs[-6:] if last else refs[-5:]
    step = pl.program_id(0)
    left = rank_masked(left_ref[...], ranks_ref[tile])
    left_out_ref[...] = jnp.concatenate([left] * 3, axis=0)
    right = rank_masked(right_ref[...], ranks_ref[tile])

    @pl.when(step == 0)
    def _():
        fold_ref[...] = refs[0][...] if last else jnp.zeros_like(fold_ref)

    for index, out_ref in enumerate((own_ref, other_ref)):
        for k in range(out_ref.shape[1] // BLOCK):
            block = owned_block(STEPS[k], index == 0)
            columns = coupling_ref[:, pl.ds(pl.multiple_of(block * BLOCK, BLOCK), BLOCK)]
            keep = pattern_ref[tile, block].astype(F32)
            keep = jnp.broadcast_to(keep, columns.shape).astype(BF16)
            out_ref[:, k * BLOCK : (k + 1) * BLOCK] = columns * keep
        fold_ref[index] += jnp.dot(right, out_ref[...], preferred_element_type=F32)

    @pl.when(step == pl.num_programs(0) - 1)
    def _():
        if last:
            for index, out_ref in enumerate(fold_out_refs):
                out_ref[...] = jnp.concatenate(split3(fold_ref[index]), axis=0)
        else:
            fold_out_refs[0][...] = fold_ref[...]


def stacked(refs):
    return jnp.concatenate([ref[...] for ref in refs], axis=0)


def member():
    return lax.rem(lax.axis_index("z"), 2) * 2 + lax.axis_index("yh")


def portion_rows(change, count):
    place = member()
    place = place + (change & 1) * (1 - 2 * lax.rem(place, 2))
    place = place + (change & 2) * (1 - 2 * lax.div(place, 2))
    return pl.ds(pl.multiple_of(place * count, count), count)


def project_kernel(own_fold_ref, other_fold_ref, *refs):
    panel_refs, out_refs, total_ref = refs[:-5], refs[-5:-1], refs[-1]
    half = len(panel_refs) // 2
    value = jnp.dot(own_fold_ref[...], stacked(panel_refs[:half]), preferred_element_type=F32)
    value += jnp.dot(
        other_fold_ref[...], stacked(panel_refs[half:]), preferred_element_type=F32
    )
    total_ref[...] = value[:RANK] + (value[RANK : 2 * RANK] + value[2 * RANK :])
    for change, out_ref in enumerate(out_refs):
        out_ref[...] = total_ref[portion_rows(change, out_ref.shape[0]), :]


def load_first_kernel(*refs):
    masked_refs, refs = refs[:TILES], refs[TILES:]
    out_ref, token_ref = refs[-2:]
    token_ref[...] = jnp.zeros_like(token_ref)
    panel = stacked(refs[:-2])
    for tile in range(out_ref.shape[0] // TILE):
        rows = slice(tile * TILE, (tile + 1) * TILE)
        out_ref[rows, :] = jnp.dot(masked_refs[tile][...], panel, preferred_element_type=F32)


def load_second_kernel(first_ref, scale_ref, *refs):
    masked_refs, refs = refs[:TILES], refs[TILES:]
    out_ref, token_ref = refs[-2:]
    token_ref[...] = jnp.zeros_like(token_ref)
    panel = stacked(refs[:-2])
    for tile in range(first_ref.shape[0] // TILE):
        rows = slice(tile * TILE, (tile + 1) * TILE)
        load = jnp.dot(masked_refs[tile][...], panel, preferred_element_type=F32)
        out_ref[:, rows] = scale_ref[:, rows] * (first_ref[rows, :] + load).T


def back_block(solved_ref, masked_refs, block):
    columns = slice(block * BLOCK, (block + 1) * BLOCK)
    masked = jnp.concatenate([ref[:, columns] for ref in masked_refs], axis=0)
    return jnp.dot(solved_ref[...], masked, preferred_element_type=F32)


def solve_back_kernel(scaled_ref, *refs):
    left_refs, masked_refs, part_refs = refs[:TILES], refs[TILES : 2 * TILES], refs[2 * TILES : -3]
    solved_ref, out_ref, projection_ref = refs[-3:]
    for change, part_ref in enumerate(part_refs):
        projection_ref[portion_rows(change, part_ref.shape[0]), :] = part_ref[...]
    pieces = jnp.concatenate(split3(projection_ref[...]), axis=0)
    for tile, left_ref in enumerate(left_refs):
        low_rank = lax.dot_general(
            pieces, left_ref[...], (((0,), (0,)), ((), ())), preferred_element_type=F32
        )
        rows = slice(tile * TILE, (tile + 1) * TILE)
        solved_ref[:, rows] = (scaled_ref[:, rows] + low_rank).astype(BF16)
    for k in range(out_ref.shape[0]):
        out_ref[k] = back_block(solved_ref, masked_refs, k).astype(BF16)


def back_kernel(solved_ref, *refs, start):
    masked_refs, out_ref = refs[:TILES], refs[-1]
    for k in range(out_ref.shape[0]):
        out_ref[k] = back_block(solved_ref, masked_refs, start + k).astype(BF16)


def back_add_kernel(solved_ref, *refs, start):
    masked_refs, given_ref, out_ref = refs[:TILES], refs[TILES], refs[-1]
    for k in range(given_ref.shape[0]):
        value = back_block(solved_ref, masked_refs, start + k) + given_ref[k].astype(F32)
        owner = lax.div(owned_block(STEPS[start + k], True), 2)
        out_ref[owner] = value.astype(BF16)


def params():
    return pltpu.CompilerParams(vmem_limit_bytes=VMEM_BYTES)


def cost(flops, size):
    return pl.CostEstimate(flops=flops, bytes_accessed=size, transcendentals=0)


def whole(shape):
    return pl.BlockSpec(shape, lambda *_: (0,) * len(shape), pipeline_mode=pl.Buffered(1))


ANYWHERE = pl.BlockSpec(memory_space=pl.ANY)
INSIDE = pl.BlockSpec(memory_space=pltpu.VMEM)


def far(value):
    return pltpu.with_memory_space_constraint(value, pltpu.HBM)


def near_by(value):
    return pltpu.with_memory_space_constraint(value, pltpu.VMEM)


def mask(pattern, ranks, coupling, right, left, tile, fold=None, after=None):
    rows, width = coupling.shape
    half = width // 2
    steps = TILE // SLAB
    last = fold is not None
    masked = jax.ShapeDtypeStruct((TILE, half), BF16)
    masked_spec = pl.BlockSpec((SLAB, half), lambda i, *_: (i, 0))
    basis_spec = pl.BlockSpec((RANK, SLAB), lambda i, *_: (0, tile * steps + i))
    if last:
        folds = [jax.ShapeDtypeStruct((3 * RANK, half), BF16)] * 2
    else:
        folds = [jax.ShapeDtypeStruct((2, RANK, half), F32)]
    more = [fold, after] if last else []
    return pl.pallas_call(
        functools.partial(mask_kernel, tile=tile, last=last),
        out_shape=[masked, masked, jax.ShapeDtypeStruct((3 * RANK, TILE), BF16)] + folds,
        grid_spec=pltpu.PrefetchScalarGridSpec(
            num_scalar_prefetch=2,
            grid=(steps,),
            in_specs=[
                pl.BlockSpec((SLAB, width), lambda i, *_: (tile * steps + i, 0)),
                basis_spec,
                basis_spec,
            ]
            + ([whole(fold.shape), ANYWHERE] if last else []),
            out_specs=[
                masked_spec, masked_spec, pl.BlockSpec((3 * RANK, SLAB), lambda i, *_: (0, i))
            ]
            + [whole(shape.shape) for shape in folds],
            scratch_shapes=[pltpu.VMEM((2, RANK, half), F32)],
        ),
        cost_estimate=cost(2 * TILE * width * RANK, 4 * TILE * width),
        compiler_params=params(),
        name="mask",
    )(far(pattern), far(ranks), far(coupling), far(right), far(left), *more)


def inside(kernel, name, out_shape, operands, flops, aliases=None, scratch=()):
    return pl.pallas_call(
        kernel,
        out_shape=out_shape,
        in_specs=[INSIDE] * len(operands),
        out_specs=jax.tree.map(lambda _: INSIDE, out_shape),
        scratch_shapes=scratch,
        input_output_aliases=aliases or {},
        cost_estimate=cost(flops, 1 << 20),
        compiler_params=params(),
        name=name,
    )(*[near_by(operand) for operand in operands])


def project(own_fold, other_fold, mine, theirs):
    vectors = mine[0].shape[1]
    part = jax.ShapeDtypeStruct((RANK // 4, vectors), F32)
    return inside(
        project_kernel, "project", [part] * 4, (own_fold, other_fold, *mine, *theirs),
        12 * own_fold.size * vectors, None, [pltpu.VMEM((RANK, vectors), F32)],
    )


def load_first(masked, panels):
    rows, depth = len(masked) * TILE, masked[0].shape[1]
    vectors = panels[0].shape[1]
    out = jax.ShapeDtypeStruct((rows, vectors), F32)
    token = jax.ShapeDtypeStruct((RANK // 4, vectors), F32)
    return inside(
        load_first_kernel, "load_first", (out, token), (*masked, *panels),
        2 * rows * depth * vectors,
    )


def load_second(masked, panels, first, scale):
    rows, depth = len(masked) * TILE, masked[0].shape[1]
    vectors = panels[0].shape[1]
    out = jax.ShapeDtypeStruct((vectors, rows), F32)
    token = jax.ShapeDtypeStruct((RANK // 4, vectors), F32)
    return inside(
        load_second_kernel, "load_second", (out, token), (first, scale, *masked, *panels),
        2 * rows * depth * vectors,
    )


def solve_back(scaled, parts, left, masked, count):
    vectors, rows = scaled.shape
    out = (
        jax.ShapeDtypeStruct((vectors, rows), BF16),
        jax.ShapeDtypeStruct((count, vectors, BLOCK), BF16),
    )
    return inside(
        solve_back_kernel, "solve_back", out, (scaled, *left, *masked, *parts),
        2 * rows * count * BLOCK * vectors, None, [pltpu.VMEM((RANK, vectors), F32)],
    )


def back(solved, masked, start, count):
    vectors, rows = solved.shape
    return inside(
        functools.partial(back_kernel, start=start), "back",
        jax.ShapeDtypeStruct((count, vectors, BLOCK), BF16), (solved, *masked),
        2 * rows * count * BLOCK * vectors,
    )


def back_add(solved, masked, start, given, into):
    vectors, rows = solved.shape
    return inside(
        functools.partial(back_add_kernel, start=start), "back_add",
        jax.ShapeDtypeStruct((len(STEPS), vectors, BLOCK), BF16),
        (solved, *masked, given, *into), 2 * rows * given.shape[0] * BLOCK * vectors,
        {2 + TILES: 0} if into else None,
    )


def exchange(value, axes):
    return lax.all_to_all(value, axes, 0, 0, tiled=True)


def swap(value):
    return lax.ppermute(value, "c", [(0, 1), (1, 0)])


def pin_kernel(*refs):
    pass


def pin(values, after):
    shapes = [jax.ShapeDtypeStruct(value.shape, value.dtype) for value in values]
    return pl.pallas_call(
        pin_kernel,
        out_shape=shapes,
        in_specs=[ANYWHERE] * (len(values) + 1),
        out_specs=[ANYWHERE] * len(values),
        input_output_aliases={k: k for k in range(len(values))},
        compiler_params=params(),
        name="pin",
    )(*values, after)


def shift(value, dx, dy, dh=0):
    wide, high, halves = [lax.axis_size(name) for name in ("x", "yl", "yh")]
    pairs = [
        (
            (x * high + y) * halves + h,
            ((x + dx) % wide * high + (y + dy) % high) * halves + (h + dh) % halves,
        )
        for x in range(wide)
        for y in range(high)
        for h in range(halves)
    ]
    return lax.ppermute(value, ("x", "yl", "yh"), pairs)


NEAR = ((0, 1), (1, 0), (1, 1))
APART = ((2, 0), (4, 0), (6, 0))


def trade(values, partners):
    layers, halves = lax.axis_size("z"), lax.axis_size("yh")
    received = []
    for value, (dz, dh) in zip(values, partners):
        pairs = [
            (z * halves + h, (z ^ dz) * halves + (h ^ dh))
            for z in range(layers)
            for h in range(halves)
        ]
        received.append(lax.ppermute(value, ("z", "yh"), pairs))
    return received


def total(value, terms, token):
    return (value + terms[0]) + (terms[1] + terms[2]) + token


def local(
    interface_panel,
    interface_block,
    coupling,
    coupling_pattern,
    tile_ranks,
    basis_left,
    basis_right,
    interior_scale,
):
    members = lax.axis_size("z") * lax.axis_size("yh")
    block_rows, vectors = interface_panel.shape
    here = interface_panel
    across, beside = shift(here, 2, 0), shift(here, 0, 1)
    behind, ahead = shift(here, 1, 0), shift(here, -1, 0)
    rest = tile_ranks[0], coupling[0], basis_right[0], basis_left[0]
    own_0, other_0, left_0, fold = mask(coupling_pattern[0], *rest, 0)
    across, beside = pin([across, beside], fold)
    corners = [shift(beside, 1, 0), shift(beside, -1, 0), shift(across, 0, 1, 1)]
    own_1, other_1, left_1, own_fold, other_fold = mask(
        coupling_pattern[0], *rest, 1, fold, beside
    )
    own, other, left = (own_0, own_1), (other_0, other_1), (left_0, left_1)
    mine = [*pin([here, beside, behind, ahead, across], left_1), *corners]
    theirs = [swap(block) for block in mine]
    keep, *others = project(own_fold, other_fold, mine, theirs)
    received = trade(others, NEAR)
    first, token_1 = load_first(own, mine)
    scaled, token_2 = load_second(other, theirs, first, interior_scale)
    keep = total(keep, received, token_1)
    keep = total(keep, trade([keep] * 3, APART), token_2)
    parts = [keep] + trade([keep] * 3, NEAR)

    half = len(STEPS) // 2
    solved, give = solve_back(scaled, parts, left, other, half)
    give_1 = swap(give)
    give_2 = swap(back(solved, other, half, half))
    term = back_add(solved, own, 0, give_1, ())
    term = back_add(solved, own, half, give_2, (term,))

    halves, layers = lax.axis_size("yh"), lax.axis_size("z")
    part, piece = vectors // halves, vectors // members
    term = term.reshape(len(STEPS) * halves, part, block_rows)
    term = jnp.sum(exchange(term, ("x", "yl", "yh")).astype(F32), axis=0)
    term = jnp.sum(exchange(term.reshape(layers, piece, block_rows), "z"), axis=0)
    term = exchange(jnp.broadcast_to(term[None], (members, piece, block_rows)), ("yh", "z"))
    coupled = term.reshape(vectors, block_rows).T
    local_image = jnp.dot(interface_block, interface_panel, preferred_element_type=F32)
    return local_image - coupled


def solution(mesh):
    shape = (4, 2, 2, 8, 2)
    fine = jax.sharding.Mesh(mesh.devices.reshape(shape), ("x", "yl", "c", "z", "yh"))
    dom, grp = ("x", "yl", "c"), ("z", "yh")
    return jax.shard_map(
        local,
        mesh=fine,
        in_specs=(
            P(dom, None),
            P(dom, None),
            P(dom, grp, None),
            P(dom, grp, None),
            P(dom, grp),
            P(dom, None, grp),
            P(dom, None, grp),
            P(dom, grp),
        ),
        out_specs=P(dom, None),
        check_vma=False,
    )
```

```python
import functools

import jax
import jax.numpy as jnp
from jax import lax
from jax.experimental import pallas as pl
from jax.experimental.pallas import tpu as pltpu
from jax.sharding import PartitionSpec as P

TILE = 512
RANK = 64
BLOCK = 256
TILES = 2
SLAB = 256
BF16 = jnp.bfloat16
F32 = jnp.float32
VMEM_BYTES = 20 * 1024 * 1024


def split3(value):
    high = value.astype(BF16)
    rest = value - high.astype(F32)
    middle = rest.astype(BF16)
    low = (rest - middle.astype(F32)).astype(BF16)
    return high, middle, low


def rank_masked(basis, rank):
    row = lax.broadcasted_iota(jnp.int32, basis.shape, 0)
    return jnp.where(row < rank, basis, jnp.zeros_like(basis))


STEPS = ((0, 0), (0, 1), (-1, 0), (1, 0), (2, 0), (-1, 1), (1, 1), (2, 1))


def owned_block(step, same_core):
    wide, high = lax.axis_size("x"), lax.axis_size("yl")
    x = lax.rem(lax.axis_index("x") + (step[0] + wide), wide)
    y = lax.rem(lax.axis_index("yl") + (step[1] + high), high)
    core = lax.axis_index("c")
    return (x * high + y) * 2 + (core if same_core else 1 - core)


def mask_kernel(pattern_ref, ranks_ref, coupling_ref, right_ref, left_ref, *refs, tile, last):
    own_ref, other_ref, left_out_ref, *fold_out_refs, fold_ref = refs[-6:] if last else refs[-5:]
    step = pl.program_id(0)
    left = rank_masked(left_ref[...], ranks_ref[tile])
    left_out_ref[...] = jnp.concatenate([left] * 3, axis=0)
    right = rank_masked(right_ref[...], ranks_ref[tile])

    @pl.when(step == 0)
    def _():
        fold_ref[...] = refs[0][...] if last else jnp.zeros_like(fold_ref)

    for index, out_ref in enumerate((own_ref, other_ref)):
        for k in range(out_ref.shape[1] // BLOCK):
            block = owned_block(STEPS[k], index == 0)
            columns = coupling_ref[:, pl.ds(pl.multiple_of(block * BLOCK, BLOCK), BLOCK)]
            keep = pattern_ref[tile, block].astype(F32)
            keep = jnp.broadcast_to(keep, columns.shape).astype(BF16)
            out_ref[:, k * BLOCK : (k + 1) * BLOCK] = columns * keep
        fold_ref[index] += jnp.dot(right, out_ref[...], preferred_element_type=F32)

    @pl.when(step == pl.num_programs(0) - 1)
    def _():
        if last:
            for index, out_ref in enumerate(fold_out_refs):
                out_ref[...] = jnp.concatenate(split3(fold_ref[index]), axis=0)
        else:
            fold_out_refs[0][...] = fold_ref[...]


def stacked(refs):
    return jnp.concatenate([ref[...] for ref in refs], axis=0)


def member():
    return lax.axis_index("zl") * 2 + lax.axis_index("yh")


def portion_rows(change, count):
    place = member()
    place = place + (change & 1) * (1 - 2 * lax.rem(place, 2))
    place = place + (change & 2) * (1 - 2 * lax.div(place, 2))
    return pl.ds(pl.multiple_of(place * count, count), count)


def project_kernel(own_fold_ref, other_fold_ref, *refs):
    panel_refs, out_refs, total_ref = refs[:-5], refs[-5:-1], refs[-1]
    half = len(panel_refs) // 2
    value = jnp.dot(own_fold_ref[...], stacked(panel_refs[:half]), preferred_element_type=F32)
    value += jnp.dot(
        other_fold_ref[...], stacked(panel_refs[half:]), preferred_element_type=F32
    )
    total_ref[...] = value[:RANK] + (value[RANK : 2 * RANK] + value[2 * RANK :])
    for change, out_ref in enumerate(out_refs):
        out_ref[...] = total_ref[portion_rows(change, out_ref.shape[0]), :]


def load_first_kernel(*refs):
    masked_refs, refs = refs[:TILES], refs[TILES:]
    out_ref, token_ref = refs[-2:]
    token_ref[...] = jnp.zeros_like(token_ref)
    panel = stacked(refs[:-2])
    for tile in range(out_ref.shape[0] // TILE):
        rows = slice(tile * TILE, (tile + 1) * TILE)
        out_ref[rows, :] = jnp.dot(masked_refs[tile][...], panel, preferred_element_type=F32)


def load_second_kernel(first_ref, scale_ref, *refs):
    masked_refs, refs = refs[:TILES], refs[TILES:]
    out_ref, token_ref = refs[-2:]
    token_ref[...] = jnp.zeros_like(token_ref)
    panel = stacked(refs[:-2])
    for tile in range(first_ref.shape[0] // TILE):
        rows = slice(tile * TILE, (tile + 1) * TILE)
        load = jnp.dot(masked_refs[tile][...], panel, preferred_element_type=F32)
        out_ref[:, rows] = scale_ref[:, rows] * (first_ref[rows, :] + load).T


def back_block(solved_ref, masked_refs, block):
    columns = slice(block * BLOCK, (block + 1) * BLOCK)
    masked = jnp.concatenate([ref[:, columns] for ref in masked_refs], axis=0)
    return jnp.dot(solved_ref[...], masked, preferred_element_type=F32)


def solve_back_kernel(scaled_ref, projection_ref, *refs):
    left_refs, masked_refs = refs[:TILES], refs[TILES : 2 * TILES]
    solved_ref, out_ref = refs[-2:]
    pieces = jnp.concatenate(split3(projection_ref[...]), axis=0)
    for tile, left_ref in enumerate(left_refs):
        low_rank = lax.dot_general(
            pieces, left_ref[...], (((0,), (0,)), ((), ())), preferred_element_type=F32
        )
        rows = slice(tile * TILE, (tile + 1) * TILE)
        solved_ref[:, rows] = (scaled_ref[:, rows] + low_rank).astype(BF16)
    for k in range(out_ref.shape[0]):
        out_ref[k] = back_block(solved_ref, masked_refs, k).astype(BF16)


def back_kernel(solved_ref, *refs, start):
    masked_refs, out_ref = refs[:TILES], refs[-1]
    for k in range(out_ref.shape[0]):
        out_ref[k] = back_block(solved_ref, masked_refs, start + k).astype(BF16)


def back_add_kernel(solved_ref, *refs, start):
    masked_refs, given_ref, out_ref = refs[:TILES], refs[TILES], refs[-1]
    for k in range(given_ref.shape[0]):
        value = back_block(solved_ref, masked_refs, start + k) + given_ref[k].astype(F32)
        owner = lax.div(owned_block(STEPS[start + k], True), 2)
        out_ref[owner] = value.astype(BF16)


def params():
    return pltpu.CompilerParams(vmem_limit_bytes=VMEM_BYTES)


def cost(flops, size):
    return pl.CostEstimate(flops=flops, bytes_accessed=size, transcendentals=0)


def whole(shape):
    return pl.BlockSpec(shape, lambda *_: (0,) * len(shape), pipeline_mode=pl.Buffered(1))


ANYWHERE = pl.BlockSpec(memory_space=pl.ANY)
INSIDE = pl.BlockSpec(memory_space=pltpu.VMEM)


def far(value):
    return pltpu.with_memory_space_constraint(value, pltpu.HBM)


def near_by(value):
    return pltpu.with_memory_space_constraint(value, pltpu.VMEM)


def mask(pattern, ranks, coupling, right, left, tile, fold=None, after=None):
    rows, width = coupling.shape
    half = width // 2
    steps = TILE // SLAB
    last = fold is not None
    masked = jax.ShapeDtypeStruct((TILE, half), BF16)
    masked_spec = pl.BlockSpec((SLAB, half), lambda i, *_: (i, 0))
    basis_spec = pl.BlockSpec((RANK, SLAB), lambda i, *_: (0, tile * steps + i))
    if last:
        folds = [jax.ShapeDtypeStruct((3 * RANK, half), BF16)] * 2
    else:
        folds = [jax.ShapeDtypeStruct((2, RANK, half), F32)]
    more = [fold, after] if last else []
    return pl.pallas_call(
        functools.partial(mask_kernel, tile=tile, last=last),
        out_shape=[masked, masked, jax.ShapeDtypeStruct((3 * RANK, TILE), BF16)] + folds,
        grid_spec=pltpu.PrefetchScalarGridSpec(
            num_scalar_prefetch=2,
            grid=(steps,),
            in_specs=[
                pl.BlockSpec((SLAB, width), lambda i, *_: (tile * steps + i, 0)),
                basis_spec,
                basis_spec,
            ]
            + ([whole(fold.shape), ANYWHERE] if last else []),
            out_specs=[
                masked_spec, masked_spec, pl.BlockSpec((3 * RANK, SLAB), lambda i, *_: (0, i))
            ]
            + [whole(shape.shape) for shape in folds],
            scratch_shapes=[pltpu.VMEM((2, RANK, half), F32)],
        ),
        cost_estimate=cost(2 * TILE * width * RANK, 4 * TILE * width),
        compiler_params=params(),
        name="mask",
    )(far(pattern), far(ranks), far(coupling), far(right), far(left), *more)


def inside(kernel, name, out_shape, operands, flops, aliases=None, scratch=()):
    return pl.pallas_call(
        kernel,
        out_shape=out_shape,
        in_specs=[INSIDE] * len(operands),
        out_specs=jax.tree.map(lambda _: INSIDE, out_shape),
        scratch_shapes=scratch,
        input_output_aliases=aliases or {},
        cost_estimate=cost(flops, 1 << 20),
        compiler_params=params(),
        name=name,
    )(*[near_by(operand) for operand in operands])


def project(own_fold, other_fold, mine, theirs):
    vectors = mine[0].shape[1]
    part = jax.ShapeDtypeStruct((RANK // 4, vectors), F32)
    return inside(
        project_kernel, "project", [part] * 4, (own_fold, other_fold, *mine, *theirs),
        12 * own_fold.size * vectors, None, [pltpu.VMEM((RANK, vectors), F32)],
    )


def load_first(masked, panels):
    rows, depth = len(masked) * TILE, masked[0].shape[1]
    vectors = panels[0].shape[1]
    out = jax.ShapeDtypeStruct((rows, vectors), F32)
    token = jax.ShapeDtypeStruct((RANK // 4, vectors), F32)
    return inside(
        load_first_kernel, "load_first", (out, token), (*masked, *panels),
        2 * rows * depth * vectors,
    )


def load_second(masked, panels, first, scale):
    rows, depth = len(masked) * TILE, masked[0].shape[1]
    vectors = panels[0].shape[1]
    out = jax.ShapeDtypeStruct((vectors, rows), F32)
    token = jax.ShapeDtypeStruct((RANK // 4, vectors), F32)
    return inside(
        load_second_kernel, "load_second", (out, token), (first, scale, *masked, *panels),
        2 * rows * depth * vectors,
    )


def solve_back(scaled, projection, left, masked, count):
    vectors, rows = scaled.shape
    out = (
        jax.ShapeDtypeStruct((vectors, rows), BF16),
        jax.ShapeDtypeStruct((count, vectors, BLOCK), BF16),
    )
    return inside(
        solve_back_kernel, "solve_back", out, (scaled, projection, *left, *masked),
        2 * rows * count * BLOCK * vectors,
    )


def back(solved, masked, start, count):
    vectors, rows = solved.shape
    return inside(
        functools.partial(back_kernel, start=start), "back",
        jax.ShapeDtypeStruct((count, vectors, BLOCK), BF16), (solved, *masked),
        2 * rows * count * BLOCK * vectors,
    )


def back_add(solved, masked, start, given, into):
    vectors, rows = solved.shape
    return inside(
        functools.partial(back_add_kernel, start=start), "back_add",
        jax.ShapeDtypeStruct((len(STEPS), vectors, BLOCK), BF16),
        (solved, *masked, given, *into), 2 * rows * given.shape[0] * BLOCK * vectors,
        {2 + TILES: 0} if into else None,
    )


def exchange(value, axes):
    return lax.all_to_all(value, axes, 0, 0, tiled=True)


def swap(value):
    return lax.ppermute(value, "c", [(0, 1), (1, 0)])


def pin_kernel(*refs):
    pass


def pin(values, after):
    shapes = [jax.ShapeDtypeStruct(value.shape, value.dtype) for value in values]
    return pl.pallas_call(
        pin_kernel,
        out_shape=shapes,
        in_specs=[ANYWHERE] * (len(values) + 1),
        out_specs=[ANYWHERE] * len(values),
        input_output_aliases={k: k for k in range(len(values))},
        compiler_params=params(),
        name="pin",
    )(*values, after)


def shift(value, dx, dy, dh=0):
    wide, high, halves = [lax.axis_size(name) for name in ("x", "yl", "yh")]
    pairs = [
        (
            (x * high + y) * halves + h,
            ((x + dx) % wide * high + (y + dy) % high) * halves + (h + dh) % halves,
        )
        for x in range(wide)
        for y in range(high)
        for h in range(halves)
    ]
    return lax.ppermute(value, ("x", "yl", "yh"), pairs)


LAYERS = ("zh", "zl")
NEAR = ((0, 1), (1, 0), (1, 1))
APART = ((4, 0), (2, 0), (6, 0))


def trade(values, partners):
    layers, halves = lax.axis_size(LAYERS), lax.axis_size("yh")
    received = []
    for value, (dz, dh) in zip(values, partners):
        pairs = [
            (z * halves + h, (z ^ dz) * halves + (h ^ dh))
            for z in range(layers)
            for h in range(halves)
        ]
        received.append(lax.ppermute(value, (*LAYERS, "yh"), pairs))
    return received


def total(value, terms, token):
    return (value + terms[0]) + (terms[1] + terms[2]) + token


def local(
    interface_panel,
    interface_block,
    coupling,
    coupling_pattern,
    tile_ranks,
    basis_left,
    basis_right,
    interior_scale,
):
    members = lax.axis_size((*LAYERS, "yh"))
    block_rows, vectors = interface_panel.shape
    here = interface_panel
    across, beside = shift(here, 2, 0), shift(here, 0, 1)
    behind, ahead = shift(here, 1, 0), shift(here, -1, 0)
    rest = tile_ranks[0], coupling[0], basis_right[0], basis_left[0]
    own_0, other_0, left_0, fold = mask(coupling_pattern[0], *rest, 0)
    across, beside = pin([across, beside], fold)
    corners = [shift(beside, 1, 0), shift(beside, -1, 0), shift(across, 0, 1, 1)]
    own_1, other_1, left_1, own_fold, other_fold = mask(
        coupling_pattern[0], *rest, 1, fold, beside
    )
    own, other, left = (own_0, own_1), (other_0, other_1), (left_0, left_1)
    mine = [*pin([here, beside, behind, ahead, across], left_1), *corners]
    theirs = [swap(block) for block in mine]
    keep, *others = project(own_fold, other_fold, mine, theirs)
    received = trade(others, NEAR)
    first, token_1 = load_first(own, mine)
    scaled, token_2 = load_second(other, theirs, first, interior_scale)
    keep = total(keep, received, token_1)
    keep = total(keep, trade([keep] * 3, APART), token_2)
    parts = jnp.broadcast_to(keep[None], (4,) + keep.shape)
    projection = exchange(parts, ("zl", "yh")).reshape(RANK, vectors)

    half = len(STEPS) // 2
    solved, give = solve_back(scaled, projection, left, other, half)
    give_1 = swap(give)
    give_2 = swap(back(solved, other, half, half))
    term = back_add(solved, own, 0, give_1, ())
    term = back_add(solved, own, half, give_2, (term,))

    halves, layers = lax.axis_size("yh"), lax.axis_size(LAYERS)
    part, piece = vectors // halves, vectors // members
    term = term.reshape(len(STEPS) * halves, part, block_rows)
    term = jnp.sum(exchange(term, ("x", "yl", "yh")).astype(F32), axis=0)
    term = jnp.sum(exchange(term.reshape(layers, piece, block_rows), LAYERS), axis=0)
    term = exchange(jnp.broadcast_to(term[None], (members, piece, block_rows)), ("yh", *LAYERS))
    coupled = term.reshape(vectors, block_rows).T
    local_image = jnp.dot(interface_block, interface_panel, preferred_element_type=F32)
    return local_image - coupled


def solution(mesh):
    dom, grp = ("x", "yl", "c"), ("zh", "zl", "yh")
    fine = jax.sharding.Mesh(mesh.devices.reshape(4, 2, 2, 4, 2, 2), dom + grp)
    return jax.shard_map(
        local,
        mesh=fine,
        in_specs=(
            P(dom, None),
            P(dom, None),
            P(dom, grp, None),
            P(dom, grp, None),
            P(dom, grp),
            P(dom, None, grp),
            P(dom, None, grp),
            P(dom, grp),
        ),
        out_specs=P(dom, None),
        check_vma=False,
    )
```

```python
import functools

import jax
import jax.numpy as jnp
from jax import lax
from jax.experimental import pallas as pl
from jax.experimental.pallas import tpu as pltpu
from jax.sharding import PartitionSpec as P

TILE = 512
RANK = 64
BLOCK = 256
TILES = 2
SLAB = 256
BF16 = jnp.bfloat16
F32 = jnp.float32
VMEM_BYTES = 20 * 1024 * 1024


def split3(value):
    high = value.astype(BF16)
    rest = value - high.astype(F32)
    middle = rest.astype(BF16)
    low = (rest - middle.astype(F32)).astype(BF16)
    return high, middle, low


def rank_masked(basis, rank):
    row = lax.broadcasted_iota(jnp.int32, basis.shape, 0)
    return jnp.where(row < rank, basis, jnp.zeros_like(basis))


STEPS = ((0, 0), (0, 1), (-1, 0), (1, 0), (2, 0), (-1, 1), (1, 1), (2, 1))


def owned_block(step, same_core):
    wide, high = lax.axis_size("x"), lax.axis_size("yl")
    x = lax.rem(lax.axis_index("x") + (step[0] + wide), wide)
    y = lax.rem(lax.axis_index("yl") + (step[1] + high), high)
    core = lax.axis_index("c")
    return (x * high + y) * 2 + (core if same_core else 1 - core)


def mask_kernel(pattern_ref, ranks_ref, coupling_ref, right_ref, left_ref, *refs, tile, last):
    own_ref, other_ref, left_out_ref, *fold_out_refs, fold_ref = refs[-6:] if last else refs[-5:]
    step = pl.program_id(0)
    left = rank_masked(left_ref[...], ranks_ref[tile])
    left_out_ref[...] = jnp.concatenate([left] * 3, axis=0)
    right = rank_masked(right_ref[...], ranks_ref[tile])

    @pl.when(step == 0)
    def _():
        fold_ref[...] = refs[0][...] if last else jnp.zeros_like(fold_ref)

    for index, out_ref in enumerate((own_ref, other_ref)):
        for k in range(out_ref.shape[1] // BLOCK):
            block = owned_block(STEPS[k], index == 0)
            columns = coupling_ref[:, pl.ds(pl.multiple_of(block * BLOCK, BLOCK), BLOCK)]
            keep = pattern_ref[tile, block].astype(F32)
            keep = jnp.broadcast_to(keep, columns.shape).astype(BF16)
            out_ref[:, k * BLOCK : (k + 1) * BLOCK] = columns * keep
        fold_ref[index] += jnp.dot(right, out_ref[...], preferred_element_type=F32)

    @pl.when(step == pl.num_programs(0) - 1)
    def _():
        if last:
            for index, out_ref in enumerate(fold_out_refs):
                out_ref[...] = jnp.concatenate(split3(fold_ref[index]), axis=0)
        else:
            fold_out_refs[0][...] = fold_ref[...]


def stacked(refs):
    return jnp.concatenate([ref[...] for ref in refs], axis=0)


def member():
    return lax.axis_index("zl") * 2 + lax.axis_index("yh")


def portion_rows(change, count):
    place = member()
    place = place + (change & 1) * (1 - 2 * lax.rem(place, 2))
    place = place + (change & 2) * (1 - 2 * lax.div(place, 2))
    return pl.ds(pl.multiple_of(place * count, count), count)


def project_kernel(own_fold_ref, other_fold_ref, *refs):
    panel_refs, out_refs, total_ref = refs[:-5], refs[-5:-1], refs[-1]
    half = len(panel_refs) // 2
    value = jnp.dot(own_fold_ref[...], stacked(panel_refs[:half]), preferred_element_type=F32)
    value += jnp.dot(
        other_fold_ref[...], stacked(panel_refs[half:]), preferred_element_type=F32
    )
    total_ref[...] = value[:RANK] + (value[RANK : 2 * RANK] + value[2 * RANK :])
    for change, out_ref in enumerate(out_refs):
        out_ref[...] = total_ref[portion_rows(change, out_ref.shape[0]), :]


def load_first_kernel(*refs):
    masked_refs, refs = refs[:TILES], refs[TILES:]
    out_ref, token_ref = refs[-2:]
    token_ref[...] = jnp.zeros_like(token_ref)
    panel = stacked(refs[:-2])
    for tile in range(out_ref.shape[0] // TILE):
        rows = slice(tile * TILE, (tile + 1) * TILE)
        out_ref[rows, :] = jnp.dot(masked_refs[tile][...], panel, preferred_element_type=F32)


def load_second_kernel(first_ref, scale_ref, *refs):
    masked_refs, refs = refs[:TILES], refs[TILES:]
    out_ref, token_ref = refs[-2:]
    token_ref[...] = jnp.zeros_like(token_ref)
    panel = stacked(refs[:-2])
    for tile in range(first_ref.shape[0] // TILE):
        rows = slice(tile * TILE, (tile + 1) * TILE)
        load = jnp.dot(masked_refs[tile][...], panel, preferred_element_type=F32)
        out_ref[:, rows] = scale_ref[:, rows] * (first_ref[rows, :] + load).T


def back_block(solved_ref, masked_refs, block):
    columns = slice(block * BLOCK, (block + 1) * BLOCK)
    masked = jnp.concatenate([ref[:, columns] for ref in masked_refs], axis=0)
    return jnp.dot(solved_ref[...], masked, preferred_element_type=F32)


def solve_back_kernel(scaled_ref, projection_ref, *refs):
    left_refs, masked_refs = refs[:TILES], refs[TILES : 2 * TILES]
    solved_ref, out_ref = refs[-2:]
    pieces = jnp.concatenate(split3(projection_ref[...]), axis=0)
    for tile, left_ref in enumerate(left_refs):
        low_rank = lax.dot_general(
            pieces, left_ref[...], (((0,), (0,)), ((), ())), preferred_element_type=F32
        )
        rows = slice(tile * TILE, (tile + 1) * TILE)
        solved_ref[:, rows] = (scaled_ref[:, rows] + low_rank).astype(BF16)
    for k in range(out_ref.shape[0]):
        out_ref[k] = back_block(solved_ref, masked_refs, k).astype(BF16)


def back_kernel(solved_ref, *refs, start):
    masked_refs, out_ref = refs[:TILES], refs[-1]
    for k in range(out_ref.shape[0]):
        out_ref[k] = back_block(solved_ref, masked_refs, start + k).astype(BF16)


def back_add_kernel(solved_ref, *refs, start):
    masked_refs, given_ref, out_ref = refs[:TILES], refs[TILES], refs[-1]
    for k in range(given_ref.shape[0]):
        value = back_block(solved_ref, masked_refs, start + k) + given_ref[k].astype(F32)
        owner = lax.div(owned_block(STEPS[start + k], True), 2)
        out_ref[owner] = value.astype(BF16)


def params():
    return pltpu.CompilerParams(vmem_limit_bytes=VMEM_BYTES)


def cost(flops, size):
    return pl.CostEstimate(flops=flops, bytes_accessed=size, transcendentals=0)


def whole(shape):
    return pl.BlockSpec(shape, lambda *_: (0,) * len(shape), pipeline_mode=pl.Buffered(1))


ANYWHERE = pl.BlockSpec(memory_space=pl.ANY)
INSIDE = pl.BlockSpec(memory_space=pltpu.VMEM)


def far(value):
    return pltpu.with_memory_space_constraint(value, pltpu.HBM)


def near_by(value):
    return pltpu.with_memory_space_constraint(value, pltpu.VMEM)


def mask(pattern, ranks, coupling, right, left, tile, fold=None, after=None):
    rows, width = coupling.shape
    half = width // 2
    steps = TILE // SLAB
    last = fold is not None
    masked = jax.ShapeDtypeStruct((TILE, half), BF16)
    masked_spec = pl.BlockSpec((SLAB, half), lambda i, *_: (i, 0))
    basis_spec = pl.BlockSpec((RANK, SLAB), lambda i, *_: (0, tile * steps + i))
    if last:
        folds = [jax.ShapeDtypeStruct((3 * RANK, half), BF16)] * 2
    else:
        folds = [jax.ShapeDtypeStruct((2, RANK, half), F32)]
    more = [fold, after] if last else []
    return pl.pallas_call(
        functools.partial(mask_kernel, tile=tile, last=last),
        out_shape=[masked, masked, jax.ShapeDtypeStruct((3 * RANK, TILE), BF16)] + folds,
        grid_spec=pltpu.PrefetchScalarGridSpec(
            num_scalar_prefetch=2,
            grid=(steps,),
            in_specs=[
                pl.BlockSpec((SLAB, width), lambda i, *_: (tile * steps + i, 0)),
                basis_spec,
                basis_spec,
            ]
            + ([whole(fold.shape), ANYWHERE] if last else []),
            out_specs=[
                masked_spec, masked_spec, pl.BlockSpec((3 * RANK, SLAB), lambda i, *_: (0, i))
            ]
            + [whole(shape.shape) for shape in folds],
            scratch_shapes=[pltpu.VMEM((2, RANK, half), F32)],
        ),
        cost_estimate=cost(2 * TILE * width * RANK, 4 * TILE * width),
        compiler_params=params(),
        name="mask",
    )(far(pattern), far(ranks), far(coupling), far(right), far(left), *more)


def inside(kernel, name, out_shape, operands, flops, aliases=None, scratch=()):
    return pl.pallas_call(
        kernel,
        out_shape=out_shape,
        in_specs=[INSIDE] * len(operands),
        out_specs=jax.tree.map(lambda _: INSIDE, out_shape),
        scratch_shapes=scratch,
        input_output_aliases=aliases or {},
        cost_estimate=cost(flops, 1 << 20),
        compiler_params=params(),
        name=name,
    )(*[near_by(operand) for operand in operands])


def project(own_fold, other_fold, mine, theirs):
    vectors = mine[0].shape[1]
    part = jax.ShapeDtypeStruct((RANK // 4, vectors), F32)
    return inside(
        project_kernel, "project", [part] * 4, (own_fold, other_fold, *mine, *theirs),
        12 * own_fold.size * vectors, None, [pltpu.VMEM((RANK, vectors), F32)],
    )


def load_first(masked, panels):
    rows, depth = len(masked) * TILE, masked[0].shape[1]
    vectors = panels[0].shape[1]
    out = jax.ShapeDtypeStruct((rows, vectors), F32)
    token = jax.ShapeDtypeStruct((RANK // 4, vectors), F32)
    return inside(
        load_first_kernel, "load_first", (out, token), (*masked, *panels),
        2 * rows * depth * vectors,
    )


def load_second(masked, panels, first, scale):
    rows, depth = len(masked) * TILE, masked[0].shape[1]
    vectors = panels[0].shape[1]
    out = jax.ShapeDtypeStruct((vectors, rows), F32)
    token = jax.ShapeDtypeStruct((RANK // 4, vectors), F32)
    return inside(
        load_second_kernel, "load_second", (out, token), (first, scale, *masked, *panels),
        2 * rows * depth * vectors,
    )


def solve_back(scaled, projection, left, masked, count):
    vectors, rows = scaled.shape
    out = (
        jax.ShapeDtypeStruct((vectors, rows), BF16),
        jax.ShapeDtypeStruct((count, vectors, BLOCK), BF16),
    )
    return inside(
        solve_back_kernel, "solve_back", out, (scaled, projection, *left, *masked),
        2 * rows * count * BLOCK * vectors,
    )


def back(solved, masked, start, count):
    vectors, rows = solved.shape
    return inside(
        functools.partial(back_kernel, start=start), "back",
        jax.ShapeDtypeStruct((count, vectors, BLOCK), BF16), (solved, *masked),
        2 * rows * count * BLOCK * vectors,
    )


def back_add(solved, masked, start, given, into):
    vectors, rows = solved.shape
    return inside(
        functools.partial(back_add_kernel, start=start), "back_add",
        jax.ShapeDtypeStruct((len(STEPS), vectors, BLOCK), BF16),
        (solved, *masked, given, *into), 2 * rows * given.shape[0] * BLOCK * vectors,
        {2 + TILES: 0} if into else None,
    )


def exchange(value, axes):
    return lax.all_to_all(value, axes, 0, 0, tiled=True)


def swap(value):
    return lax.ppermute(value, "c", [(0, 1), (1, 0)])


def pin_kernel(*refs):
    pass


def pin(values, after):
    shapes = [jax.ShapeDtypeStruct(value.shape, value.dtype) for value in values]
    return pl.pallas_call(
        pin_kernel,
        out_shape=shapes,
        in_specs=[ANYWHERE] * (len(values) + 1),
        out_specs=[ANYWHERE] * len(values),
        input_output_aliases={k: k for k in range(len(values))},
        compiler_params=params(),
        name="pin",
    )(*values, after)


def shift(value, dx, dy, dh=0):
    wide, high, halves = [lax.axis_size(name) for name in ("x", "yl", "yh")]
    pairs = [
        (
            (x * high + y) * halves + h,
            ((x + dx) % wide * high + (y + dy) % high) * halves + (h + dh) % halves,
        )
        for x in range(wide)
        for y in range(high)
        for h in range(halves)
    ]
    return lax.ppermute(value, ("x", "yl", "yh"), pairs)


LAYERS = ("zh", "zl")
NEAR = ((0, 1), (1, 0), (1, 1))
APART = ((4, 0), (2, 0), (6, 0))


def trade(values, partners):
    layers, halves = lax.axis_size(LAYERS), lax.axis_size("yh")
    received = []
    for value, (dz, dh) in zip(values, partners):
        pairs = [
            (z * halves + h, (z ^ dz) * halves + (h ^ dh))
            for z in range(layers)
            for h in range(halves)
        ]
        received.append(lax.ppermute(value, (*LAYERS, "yh"), pairs))
    return received


def total(value, terms, token):
    return (value + terms[0]) + (terms[1] + terms[2]) + token


def local(
    interface_panel,
    interface_block,
    coupling,
    coupling_pattern,
    tile_ranks,
    basis_left,
    basis_right,
    interior_scale,
):
    members = lax.axis_size((*LAYERS, "yh"))
    block_rows, vectors = interface_panel.shape
    here = interface_panel
    across, beside = shift(here, 2, 0), shift(here, 0, 1)
    behind, ahead = shift(here, 1, 0), shift(here, -1, 0)
    rest = tile_ranks[0], coupling[0], basis_right[0], basis_left[0]
    own_0, other_0, left_0, fold = mask(coupling_pattern[0], *rest, 0)
    across, beside = pin([across, beside], fold)
    corners = [shift(beside, 1, 0), shift(beside, -1, 0), shift(across, 0, 1, 1)]
    own_1, other_1, left_1, own_fold, other_fold = mask(
        coupling_pattern[0], *rest, 1, fold, beside
    )
    own, other, left = (own_0, own_1), (other_0, other_1), (left_0, left_1)
    mine = [*pin([here, beside, behind, ahead, across], left_1), *corners]
    theirs = [swap(block) for block in mine]
    keep, *others = project(own_fold, other_fold, mine, theirs)
    received = trade(others[::-1], NEAR[::-1])
    first, token_1 = load_first(own, mine)
    scaled, token_2 = load_second(other, theirs, first, interior_scale)
    keep = total(keep, received, token_1)
    keep = total(keep, trade([keep] * 3, APART), token_2)
    parts = jnp.broadcast_to(keep[None], (4,) + keep.shape)
    projection = exchange(parts, ("zl", "yh")).reshape(RANK, vectors)

    half = len(STEPS) // 2
    solved, give = solve_back(scaled, projection, left, other, half)
    give_1 = swap(give)
    give_2 = swap(back(solved, other, half, half))
    term = back_add(solved, own, 0, give_1, ())
    term = back_add(solved, own, half, give_2, (term,))

    halves, layers = lax.axis_size("yh"), lax.axis_size(LAYERS)
    part, piece = vectors // halves, vectors // members
    term = term.reshape(len(STEPS) * halves, part, block_rows)
    term = jnp.sum(exchange(term, ("x", "yl", "yh")).astype(F32), axis=0)
    term = jnp.sum(exchange(term.reshape(layers, piece, block_rows), LAYERS), axis=0)
    term = exchange(jnp.broadcast_to(term[None], (members, piece, block_rows)), ("yh", *LAYERS))
    coupled = term.reshape(vectors, block_rows).T
    local_image = jnp.dot(interface_block, interface_panel, preferred_element_type=F32)
    return local_image - coupled


def solution(mesh):
    dom, grp = ("x", "yl", "c"), ("zh", "zl", "yh")
    fine = jax.sharding.Mesh(mesh.devices.reshape(4, 2, 2, 4, 2, 2), dom + grp)
    return jax.shard_map(
        local,
        mesh=fine,
        in_specs=(
            P(dom, None),
            P(dom, None),
            P(dom, grp, None),
            P(dom, grp, None),
            P(dom, grp),
            P(dom, None, grp),
            P(dom, None, grp),
            P(dom, grp),
        ),
        out_specs=P(dom, None),
        check_vma=False,
    )
```
